32 devices in a mesh: gx: 4 (over y, x), gy: 8 (over z, core).
Axes of the slice: x: 2, y: 2, z: 4, core: 2. Of those that a mesh axis runs over, the one named last changes fastest.
Arguments:
- vectors: float32 [16, 13, 16, 1024], P(None, None, 'gx', 'gy'), may hold values from -6 to 6
- features: bfloat16 [128, 16, 1024], P(None, 'gx', 'gy'), may hold values from -6 to 6
- gains: float32 [25, 128], replicated, may hold values from 0.25 to 1.5
- edge_weight: bfloat16 [128, 169], replicated, may hold values from -0.01953125 to 0.01953125
- energies: float32 [13, 3], replicated, may hold values from -0.5 to 0.5
- neighbours: int32 [12, 16, 1024], P(None, 'gx', 'gy'), may hold values from -1 to 24, as said below
- species: int32 [16, 1024], P('gx', 'gy'), may hold values from 0 to 2
Outputs:
- evolved: float32 [16, 13, 16, 1024], P(None, None, 'gx', 'gy')
The draws below stay inside these ranges and needn't reach their ends.
Inputs may be any that keep to these rules, and one draw needn't show every extreme that they name: `neighbours`: code c names the atom c // 5 - 2 rows and c % 5 - 2 columns away on the periodic slab; 12 never appears; one atom's codes are distinct; -1 marks an empty slot.
All inputs are finite; a program needn't handle non-finite values.
Results may differ from the reference program's by a relative error of at most 0.009.
Values may be sent and summed in bfloat16 or wider, within the bound.
A program may use at most 64 MiB of HBM per device.

```python
import jax
import jax.numpy as jnp
from jax import lax

ORB = 13
FEAT = 128
VECS = 16
STEPS = 4
SLOTS = 12
CODES = 25
KINDS = 3
NX = 16
NY = 1024


def draw_neighbours(key, part):
    order_key = jax.random.fold_in(key, 11)
    empty_key = jax.random.fold_in(key, 29)
    scores = jax.random.randint(order_key, (CODES - 1, NX, NY), 0, 1 << 20) * 32 + jnp.arange(CODES - 1, dtype=jnp.int32)[:, None, None]
    ranked = jnp.argsort(scores, axis=0, stable=True)[:SLOTS].astype(jnp.int32)
    chosen = ranked + (ranked >= 12).astype(jnp.int32)
    is_empty = jax.random.randint(empty_key, (SLOTS, NX, NY), 0, 6) == 0
    return jnp.where(is_empty, -1, chosen).astype(jnp.int32)


def plant(values, own_key, least, high):
    dims = values.shape
    spot = [jax.random.randint(jax.random.fold_in(own_key, axis), (), 0, dims[axis]) for axis in range(len(dims))]
    values = values.at[tuple(spot)].set(least)
    longest = dims.index(max(dims))
    spot[longest] = (spot[longest] + 1) % dims[longest]
    return values.at[tuple(spot)].set(high)


def steps_of(rng, dims, split, low, high):
    loudness, own = 1.0, jax.random.fold_in(rng, 6)
    for dim, parts in split:
        heights = jnp.exp(jax.random.uniform(jax.random.fold_in(own, dim), (parts,), jnp.float32, low / len(split), high / len(split)))
        loudness = loudness * jnp.repeat(heights, dims[dim] // parts).reshape([-1 if axis == dim else 1 for axis in range(len(dims))])
    return loudness


def gaussian(own_key, dims, spread, bound, shards=(), kind=jnp.bfloat16):
    drawn = spread * jax.random.normal(own_key, dims, jnp.float32)
    if shards:
        drawn = drawn * steps_of(own_key, dims, shards, -0.22, 0.18)
    return jnp.clip(drawn, -bound, bound).astype(kind)


def setup_inputs(seed: int = 0) -> dict:
    streams_of = jax.random.split(jax.random.key(seed), 8)
    vectors = gaussian(streams_of[0], (VECS, ORB, NX, NY), 1.0, 6.0, ((2, 4), (3, 8)), jnp.float32)
    features = gaussian(streams_of[1], (FEAT, NX, NY), 1.0, 6.0, ((1, 4), (2, 8)))
    gains = jnp.clip(jax.random.uniform(streams_of[2], (CODES, FEAT), jnp.float32, 0.25, 1.5), 0.25, 1.5)
    edge_weight = gaussian(streams_of[3], (FEAT, ORB * ORB), (FEAT * 624) ** -0.5, 0.01953125)
    energies = jnp.clip(jax.random.uniform(streams_of[4], (ORB, KINDS), jnp.float32, -0.5, 0.5), -0.5, 0.5)
    neighbours = draw_neighbours(jax.random.fold_in(streams_of[7], 71), 0)
    species = plant(jax.random.randint(streams_of[6], (NX, NY), 0, KINDS), jax.random.fold_in(streams_of[6], 1), 0, KINDS - 1).astype(jnp.int32)
    return {"vectors": vectors, "features": features, "gains": gains, "edge_weight": edge_weight, "energies": energies, "neighbours": neighbours, "species": species}


def slot_codes(neighbours):
    centre = jnp.full((1, neighbours.shape[1], neighbours.shape[2]), 12, jnp.int32)
    listed = jnp.concatenate([neighbours, centre], axis=0)
    is_valid = listed >= 0
    return jnp.where(is_valid, listed, 12).astype(jnp.int32), is_valid


def reference(vectors, features, gains, edge_weight, energies, neighbours, species):
    code_grid, is_valid = slot_codes(neighbours)
    slot_total = code_grid.shape[0]
    row_ids = jnp.arange(NX, dtype=jnp.int32)[:, None]
    col_ids = jnp.arange(NY, dtype=jnp.int32)[None, :]
    atom_count = NX * NY
    flattened = features.reshape(FEAT, atom_count)
    self_feat = flattened.astype(jnp.float32)
    onsite = energies[:, species.reshape(atom_count)]
    identity = jnp.eye(ORB, dtype=jnp.float32)
    blocks = []
    targets = []
    for which_slot in range(slot_total):
        slot_code = code_grid[which_slot]
        shift_x = slot_code // 5 - 2
        shift_y = slot_code % 5 - 2
        target = (((row_ids + shift_x) % NX) * NY + (col_ids + shift_y) % NY).reshape(atom_count).astype(jnp.int32)
        peer_feat = jnp.take(flattened, target, axis=1).astype(jnp.float32)
        gain_rows = gains[slot_code.reshape(atom_count)].T
        edge_feat = (self_feat * peer_feat * gain_rows).astype(jnp.bfloat16)
        block_vals = jnp.dot(edge_weight.T, edge_feat, preferred_element_type=jnp.float32)
        block_vals = block_vals * is_valid[which_slot].reshape(1, atom_count).astype(jnp.float32)
        if which_slot == slot_total - 1:
            block_vals = block_vals + (identity[:, :, None] * onsite[:, None, :]).reshape(ORB * ORB, atom_count)
        blocks.append(block_vals.astype(jnp.bfloat16).reshape(ORB, ORB, atom_count))
        targets.append(target)

    def apply_hamiltonian(rounded):
        accumulated = jnp.zeros((VECS, ORB, atom_count), jnp.float32)
        for which_slot in range(slot_total):
            gathered = jnp.take(rounded, targets[which_slot], axis=2).astype(jnp.float32)
            accumulated = accumulated + jnp.einsum('abn,mbn->man', blocks[which_slot].astype(jnp.float32), gathered, precision=lax.Precision.HIGHEST)
        return accumulated

    previous = vectors.reshape(VECS, ORB, atom_count)
    current = apply_hamiltonian(previous.astype(jnp.bfloat16))
    for iteration in range(1, STEPS):
        following = 2.0 * apply_hamiltonian(current.astype(jnp.bfloat16)) - previous
        previous, current = current, following
    return current.reshape(VECS, ORB, NX, NY)
```

```python
import functools

import jax
import jax.numpy as jnp
from jax import lax
from jax.experimental import pallas as pl
from jax.experimental.pallas import tpu as pltpu
from jax.sharding import PartitionSpec as P

STEPS = 4
CODES = 25
LANES = 128
MESH = pl.DeviceIdType.MESH
ROUTES = ((-1, 0), (1, 0), (0, -1), (-1, -1), (1, -1), (0, 1), (-1, 1), (1, 1))


def neighbour_id(offset):
    place = {}
    for name, step in zip(("gx", "gy"), offset):
        count = lax.axis_size(name)
        place[name] = lax.rem(lax.axis_index(name) + step + count, count)
    return place


def lane_ids(rows, width):
    return lax.broadcasted_iota(jnp.int32, (rows, width), 1)


def exchange(sources, targets, send_sem, recv_sem, which):
    copies = []
    for route, offset in enumerate(ROUTES):
        copy = pltpu.make_async_remote_copy(
            src_ref=sources[route],
            dst_ref=targets[route],
            send_sem=send_sem.at[which, route],
            recv_sem=recv_sem.at[which, route],
            device_id=neighbour_id(offset),
            device_id_type=MESH,
        )
        copy.start()
        copies.append(copy)
    return copies


def shifts(centre, left, right):
    rows, width = centre.shape
    ids = lane_ids(rows, LANES)
    first = centre[:, :LANES]
    last = centre[:, width - LANES :]

    def before(count):
        edge = jnp.where(ids >= LANES - count, left, last)
        if width > LANES:
            edge = jnp.concatenate([centre[:, : width - LANES], edge], axis=1)
        return pltpu.roll(edge, count, 1)

    def after(count):
        edge = jnp.where(ids < count, right, first)
        if width > LANES:
            edge = jnp.concatenate([edge, centre[:, LANES:]], axis=1)
        return pltpu.roll(edge, width - count, 1)

    return [before(2), before(1), centre, after(1), after(2)]


def kernel(
    orbits,
    groups,
    vec_ref,
    feat_ref,
    gain_ref,
    weight_ref,
    onsite_ref,
    near_ref,
    out_ref,
    blk,
    moved,
    state,
    feat_moved,
    mm,
    tmp,
    feat_cols,
    feat_rows_in,
    feat_cols_in,
    rows_out,
    cols_out,
    rows_in,
    cols_in,
    side,
    send_sem,
    recv_sem,
):
    width = vec_ref.shape[2]
    chunks = width // LANES
    fields = groups * orbits
    entries = orbits * orbits
    f32, bf16 = jnp.float32, jnp.bfloat16

    barrier = pltpu.get_barrier_semaphore()
    for offset in ROUTES:
        pl.semaphore_signal(barrier, inc=1, device_id=neighbour_id(offset), device_id_type=MESH)
    pl.semaphore_wait(barrier, len(ROUTES))

    ids = lane_ids(feat_ref.shape[1], LANES)
    low_cols = jnp.zeros(ids.shape, f32)
    high_cols = jnp.zeros(ids.shape, f32)
    for row in range(4):
        held = (ids >= 2 * row) & (ids < 2 * row + 2)
        low = feat_ref[row, :, :LANES].astype(f32)
        high = feat_ref[row, :, width - LANES :].astype(f32)
        low_cols = jnp.where(held, pltpu.roll(low, 2 * row, 1) if row else low, low_cols)
        high_cols = jnp.where(held, pltpu.roll(high, 2 * row + 2, 1), high_cols)
    feat_cols[0] = low_cols.astype(bf16)
    feat_cols[1] = high_cols.astype(bf16)
    feat_copies = exchange(
        [feat_ref.at[pl.ds(0, 2)], feat_ref.at[pl.ds(2, 2)]]
        + [feat_cols.at[0]] * 3
        + [feat_cols.at[1]] * 3,
        [feat_rows_in.at[0], feat_rows_in.at[1]] + [feat_cols_in.at[k] for k in range(6)],
        send_sem,
        recv_sem,
        0,
    )

    def send_state(current, step):
        ids16 = lane_ids(16, LANES)

        def pack(pair, cols):
            low_cols, high_cols = cols
            a = current[2 * pair]
            b = current[2 * pair + 1]
            rows_out[step, 0, pair] = jnp.concatenate([a[0:8], b[0:8]], axis=0).astype(bf16)
            rows_out[step, 1, pair] = jnp.concatenate([a[8:16], b[8:16]], axis=0).astype(bf16)
            for half, tile in enumerate((a, b)):
                spot = 4 * pair + 2 * half
                held = (ids16 >= spot) & (ids16 < spot + 2)
                low_cols = jnp.where(held, pltpu.roll(tile[:, :LANES], spot, 1), low_cols)
                high_cols = jnp.where(
                    held, pltpu.roll(tile[:, width - LANES :], lax.rem(spot + 2, LANES), 1), high_cols
                )
            return low_cols, high_cols

        zero = jnp.zeros((16, LANES), f32)
        low_cols, high_cols = lax.fori_loop(0, fields // 2, pack, (zero, zero))
        cols_out[step, 0] = low_cols.astype(bf16)
        cols_out[step, 1] = high_cols.astype(bf16)
        return exchange(
            [rows_out.at[step, 0], rows_out.at[step, 1]]
            + [cols_out.at[step, 0]] * 3
            + [cols_out.at[step, 1]] * 3,
            [rows_in.at[step, 0], rows_in.at[step, 1]] + [cols_in.at[step, k] for k in range(6)],
            send_sem,
            recv_sem,
            step + 1,
        )

    copies = send_state(vec_ref, 0)

    for copy in feat_copies:
        copy.wait()
    for row in range(8):
        if row < 2:
            tile, which, spot = feat_rows_in[1, row], 2, row + 2
        elif row < 6:
            tile, which, spot = feat_ref[row - 2], 0, row - 2
        else:
            tile, which, spot = feat_rows_in[0, row - 6], 1, row - 6
        right = pltpu.roll(feat_cols_in[which].astype(f32), (LANES - 2 * spot) % LANES, 1) if spot else feat_cols_in[which].astype(f32)
        left = pltpu.roll(feat_cols_in[3 + which].astype(f32), LANES - 2 - 2 * spot, 1)
        for shift, moved_tile in enumerate(shifts(tile.astype(f32), left, right)):
            feat_moved[shift, row] = moved_tile.astype(bf16)

    sub8 = lax.broadcasted_iota(jnp.int32, (8, width), 0) < 4

    def build(code, carry):
        code_x = code // 5
        code_y = code - 5 * code_x
        present = jnp.where(code == 12, jnp.ones((4, width), f32), jnp.zeros((4, width), f32))
        for slot in range(near_ref.shape[0]):
            present = jnp.where(near_ref[slot] == code, 1.0, present)
        turned = pltpu.roll(gain_ref[...], lax.rem(LANES - code, LANES), 1)
        gain = jnp.broadcast_to(turned[:, 0:1], (turned.shape[0], width))
        for row in range(4):
            own = feat_ref[row].astype(f32)
            peer = feat_moved[code_y, code_x + row].astype(f32)
            edge = own * peer * gain * present[row : row + 1]
            mm[row] = jnp.dot(weight_ref[...], edge.astype(bf16), preferred_element_type=f32)

        @pl.when(code == 12)
        def _():
            for row in range(4):
                for orbit in range(orbits):
                    spot = orbit * (orbits + 1)
                    mm[row, pl.ds(spot, 1), :] += onsite_ref[row, pl.ds(orbit, 1), :]

        def expand(orbit, inner):
            for other in range(orbits):
                spot = orbit * orbits + other
                lines = [
                    jnp.broadcast_to(mm[row, pl.ds(spot, 1), :], (8, width)) for row in range(4)
                ]
                top = jnp.where(sub8, lines[0], lines[1])
                low = jnp.where(sub8, lines[2], lines[3])
                blk[code * entries + spot] = jnp.concatenate([top, low], axis=0).astype(bf16)
            return inner

        lax.fori_loop(0, orbits, expand, 0)
        return carry

    lax.fori_loop(0, CODES, build, 0)

    tiles = []
    start = 0
    while start < orbits:
        size = 4 if (orbits - start) % 3 else 3
        tiles.append((start, min(size, orbits - start)))
        start += size

    for step in range(STEPS):
        current = vec_ref if step == 0 else state.at[(step - 1) % 2]
        for copy in copies:
            copy.wait()
        for which, base in enumerate((3, 0)):
            side[which, 0:8] = cols_in[step, base + 2].astype(f32)[8:16]
            side[which, 8:24] = cols_in[step, base].astype(f32)
            side[which, 24:32] = cols_in[step, base + 1].astype(f32)[0:8]

        def spread(pair, carry):
            above = rows_in[step, 1, pair].astype(f32)
            below = rows_in[step, 0, pair].astype(f32)
            for half in range(2):
                field = 2 * pair + half
                spot = 2 * field
                centre = jnp.concatenate(
                    [above[8 * half : 8 * half + 8], current[field], below[8 * half : 8 * half + 8]],
                    axis=0,
                )
                left = pltpu.roll(side[0], lax.rem(LANES - 2 - spot + LANES, LANES), 1)
                right = pltpu.roll(side[1], lax.rem(LANES - spot, LANES), 1)
                for shift, tile in enumerate(shifts(centre, left, right)):
                    for chunk in range(chunks):
                        cols = slice(chunk * LANES, (chunk + 1) * LANES)
                        tmp[half, shift, chunk] = tile[:, cols]
                        for lift in range(5):
                            moved[lift * 5 + shift, field, :, cols] = tmp[
                                half, shift, chunk, 4 * lift : 4 * lift + 16
                            ].astype(bf16)
            return carry

        lax.fori_loop(0, fields // 2, spread, 0)

        target = out_ref if step == STEPS - 1 else state.at[step % 2]
        previous = vec_ref if step == 1 else state.at[step % 2]
        for chunk in range(chunks):
            cols = slice(chunk * LANES, (chunk + 1) * LANES)
            for start, size in tiles:

                def gather(code, sums):
                    parts = [[None, None] for _ in range(size * groups)]
                    for other in range(orbits):
                        chain = 0 if other < 7 else 1
                        fields_in = [moved[code, g * orbits + other, :, cols] for g in range(groups)]
                        for k in range(size):
                            entry = blk[code * entries + (start + k) * orbits + other, :, cols]
                            for g in range(groups):
                                part = parts[k * groups + g]
                                term = entry * fields_in[g]
                                part[chain] = term if part[chain] is None else part[chain] + term
                    return tuple(
                        total + (part[0] + part[1]).astype(f32) for total, part in zip(sums, parts)
                    )

                zero = jnp.zeros((16, LANES), f32)
                sums = lax.fori_loop(0, CODES, gather, (zero,) * (size * groups))
                for k in range(size):
                    for g in range(groups):
                        field = g * orbits + start + k
                        value = sums[k * groups + g]
                        if step:
                            value = 2.0 * value - previous[field, :, cols]
                        target[field, :, cols] = value
        if step < STEPS - 1:
            copies = send_state(target, step + 1)


def body(vectors, features, gains, edge_weight, energies, neighbours, species):
    count, orbits, rows, width = vectors.shape
    groups = count // 4
    channels = features.shape[0]
    entries = orbits * orbits
    padded = -(-entries // 16) * 16
    fields = groups * orbits
    f32, bf16 = jnp.float32, jnp.bfloat16
    vec = vectors.reshape(groups, 4, orbits, rows, width).transpose(0, 2, 3, 1, 4)
    vec = vec.reshape(fields, rows * 4, width)
    feat = features.transpose(1, 0, 2)
    gain = jnp.pad(gains.T, ((0, 0), (0, LANES - gains.shape[0])))
    weight = jnp.pad(edge_weight.T, ((0, padded - entries), (0, 0)))
    onsite = jnp.zeros((rows, orbits, width), f32)
    for kind in range(energies.shape[1]):
        onsite = jnp.where(species[:, None] == kind, energies[:, kind][None, :, None], onsite)
    vmem = pl.BlockSpec(memory_space=pltpu.VMEM)
    out = pl.pallas_call(
        functools.partial(kernel, orbits, groups),
        out_shape=jax.ShapeDtypeStruct(vec.shape, f32),
        in_specs=[vmem] * 6,
        out_specs=vmem,
        scratch_shapes=[
            pltpu.VMEM((CODES * entries, 16, width), bf16),
            pltpu.VMEM((CODES, fields, 16, width), bf16),
            pltpu.VMEM((2, fields, 16, width), f32),
            pltpu.VMEM((5, rows + 4, channels, width), bf16),
            pltpu.VMEM((rows, padded, width), f32),
            pltpu.VMEM((2, 5, width // LANES, 32, LANES), f32),
            pltpu.VMEM((2, channels, LANES), bf16),
            pltpu.VMEM((2, 2, channels, width), bf16),
            pltpu.VMEM((6, channels, LANES), bf16),
            pltpu.VMEM((STEPS, 2, fields // 2, 16, width), bf16),
            pltpu.VMEM((STEPS, 2, 16, LANES), bf16),
            pltpu.VMEM((STEPS, 2, fields // 2, 16, width), bf16),
            pltpu.VMEM((STEPS, 6, 16, LANES), bf16),
            pltpu.VMEM((2, 32, LANES), f32),
            pltpu.SemaphoreType.DMA((STEPS + 1, len(ROUTES))),
            pltpu.SemaphoreType.DMA((STEPS + 1, len(ROUTES))),
        ],
        compiler_params=pltpu.CompilerParams(
            collective_id=0, has_side_effects=True, vmem_limit_bytes=62 * 1024 * 1024
        ),
        cost_estimate=pl.CostEstimate(
            flops=STEPS * 2 * CODES * entries * count * rows * width,
            bytes_accessed=4 * 1024 * 1024,
            transcendentals=0,
        ),
    )(vec, feat, gain, weight, onsite, neighbours)
    out = out.reshape(groups, orbits, rows, 4, width).transpose(0, 3, 1, 2, 4)
    return out.reshape(vectors.shape)


def solution(mesh):
    return jax.shard_map(
        body,
        mesh=mesh,
        in_specs=(
            P(None, None, "gx", "gy"),
            P(None, "gx", "gy"),
            P(),
            P(),
            P(),
            P(None, "gx", "gy"),
            P("gx", "gy"),
        ),
        out_specs=P(None, None, "gx", "gy"),
        check_vma=False,
    )
```

```python
import functools

import jax
import jax.numpy as jnp
from jax import lax
from jax.experimental import pallas as pl
from jax.experimental.pallas import tpu as pltpu
from jax.sharding import PartitionSpec as P

STEPS = 4
CODES = 25
LANES = 128
MESH = pl.DeviceIdType.MESH
ROUTES = ((-1, 0), (1, 0), (0, -1), (-1, -1), (1, -1), (0, 1), (-1, 1), (1, 1))


def neighbour_id(offset):
    place = {}
    for name, step in zip(("gx", "gy"), offset):
        count = lax.axis_size(name)
        place[name] = lax.rem(lax.axis_index(name) + step + count, count)
    return place


def lane_ids(rows, width):
    return lax.broadcasted_iota(jnp.int32, (rows, width), 1)


def exchange(sources, targets, send_sem, recv_sem, which):
    copies = []
    for route, offset in enumerate(ROUTES):
        copy = pltpu.make_async_remote_copy(
            src_ref=sources[route],
            dst_ref=targets[route],
            send_sem=send_sem.at[which, route],
            recv_sem=recv_sem.at[which, route],
            device_id=neighbour_id(offset),
            device_id_type=MESH,
        )
        copy.start()
        copies.append(copy)
    return copies


def shifts(centre, left, right):
    rows, width = centre.shape
    ids = lane_ids(rows, LANES)
    first = centre[:, :LANES]
    last = centre[:, width - LANES :]

    def before(count):
        edge = jnp.where(ids >= LANES - count, left, last)
        if width > LANES:
            edge = jnp.concatenate([centre[:, : width - LANES], edge], axis=1)
        return pltpu.roll(edge, count, 1)

    def after(count):
        edge = jnp.where(ids < count, right, first)
        if width > LANES:
            edge = jnp.concatenate([edge, centre[:, LANES:]], axis=1)
        return pltpu.roll(edge, width - count, 1)

    return [before(2), before(1), centre, after(1), after(2)]


def kernel(
    orbits,
    groups,
    vec_ref,
    feat_ref,
    gain_ref,
    weight_ref,
    onsite_ref,
    near_ref,
    out_ref,
    blk,
    moved,
    state,
    feat_moved,
    mm,
    tmp,
    feat_cols,
    feat_rows_in,
    feat_cols_in,
    rows_out,
    cols_out,
    rows_in,
    cols_in,
    side,
    send_sem,
    recv_sem,
):
    width = vec_ref.shape[2]
    chunks = width // LANES
    fields = groups * orbits
    entries = orbits * orbits
    f32, bf16 = jnp.float32, jnp.bfloat16

    barrier = pltpu.get_barrier_semaphore()
    for offset in ROUTES:
        pl.semaphore_signal(barrier, inc=1, device_id=neighbour_id(offset), device_id_type=MESH)
    pl.semaphore_wait(barrier, len(ROUTES))

    ids = lane_ids(feat_ref.shape[1], LANES)
    low_cols = jnp.zeros(ids.shape, f32)
    high_cols = jnp.zeros(ids.shape, f32)
    for row in range(4):
        held = (ids >= 2 * row) & (ids < 2 * row + 2)
        low = feat_ref[row, :, :LANES].astype(f32)
        high = feat_ref[row, :, width - LANES :].astype(f32)
        low_cols = jnp.where(held, pltpu.roll(low, 2 * row, 1) if row else low, low_cols)
        high_cols = jnp.where(held, pltpu.roll(high, 2 * row + 2, 1), high_cols)
    feat_cols[0] = low_cols.astype(bf16)
    feat_cols[1] = high_cols.astype(bf16)
    feat_copies = exchange(
        [feat_ref.at[pl.ds(0, 2)], feat_ref.at[pl.ds(2, 2)]]
        + [feat_cols.at[0]] * 3
        + [feat_cols.at[1]] * 3,
        [feat_rows_in.at[0], feat_rows_in.at[1]] + [feat_cols_in.at[k] for k in range(6)],
        send_sem,
        recv_sem,
        0,
    )

    def send_state(current, step):
        ids16 = lane_ids(16, LANES)

        def pack(pair, cols):
            low_cols, high_cols = cols
            a = current[2 * pair]
            b = current[2 * pair + 1]
            rows_out[step, 0, pair] = jnp.concatenate([a[0:8], b[0:8]], axis=0).astype(bf16)
            rows_out[step, 1, pair] = jnp.concatenate([a[8:16], b[8:16]], axis=0).astype(bf16)
            for half, tile in enumerate((a, b)):
                spot = 4 * pair + 2 * half
                held = (ids16 >= spot) & (ids16 < spot + 2)
                low_cols = jnp.where(held, pltpu.roll(tile[:, :LANES], spot, 1), low_cols)
                high_cols = jnp.where(
                    held, pltpu.roll(tile[:, width - LANES :], lax.rem(spot + 2, LANES), 1), high_cols
                )
            return low_cols, high_cols

        zero = jnp.zeros((16, LANES), f32)
        low_cols, high_cols = lax.fori_loop(0, fields // 2, pack, (zero, zero))
        cols_out[step, 0] = low_cols.astype(bf16)
        cols_out[step, 1] = high_cols.astype(bf16)
        return exchange(
            [rows_out.at[step, 0], rows_out.at[step, 1]]
            + [cols_out.at[step, 0]] * 3
            + [cols_out.at[step, 1]] * 3,
            [rows_in.at[step, 0], rows_in.at[step, 1]] + [cols_in.at[step, k] for k in range(6)],
            send_sem,
            recv_sem,
            step + 1,
        )

    copies = send_state(vec_ref, 0)

    for copy in feat_copies:
        copy.wait()
    for row in range(8):
        if row < 2:
            tile, which, spot = feat_rows_in[1, row], 2, row + 2
        elif row < 6:
            tile, which, spot = feat_ref[row - 2], 0, row - 2
        else:
            tile, which, spot = feat_rows_in[0, row - 6], 1, row - 6
        right = pltpu.roll(feat_cols_in[which].astype(f32), (LANES - 2 * spot) % LANES, 1) if spot else feat_cols_in[which].astype(f32)
        left = pltpu.roll(feat_cols_in[3 + which].astype(f32), LANES - 2 - 2 * spot, 1)
        for shift, moved_tile in enumerate(shifts(tile.astype(f32), left, right)):
            feat_moved[shift, row] = moved_tile.astype(bf16)

    sub8 = lax.broadcasted_iota(jnp.int32, (8, width), 0) < 4

    def build(code, carry):
        code_x = code // 5
        code_y = code - 5 * code_x
        present = jnp.where(code == 12, jnp.ones((4, width), f32), jnp.zeros((4, width), f32))
        for slot in range(near_ref.shape[0]):
            present = jnp.where(near_ref[slot] == code, 1.0, present)
        turned = pltpu.roll(gain_ref[...], lax.rem(LANES - code, LANES), 1)
        gain = jnp.broadcast_to(turned[:, 0:1], (turned.shape[0], width))
        for row in range(4):
            own = feat_ref[row].astype(f32)
            peer = feat_moved[code_y, code_x + row].astype(f32)
            edge = own * peer * gain * present[row : row + 1]
            mm[row] = jnp.dot(weight_ref[...], edge.astype(bf16), preferred_element_type=f32)

        @pl.when(code == 12)
        def _():
            for row in range(4):
                for orbit in range(orbits):
                    spot = orbit * (orbits + 1)
                    mm[row, pl.ds(spot, 1), :] += onsite_ref[row, pl.ds(orbit, 1), :]

        for spot in range(entries):
            lines = [jnp.broadcast_to(mm[row, spot : spot + 1, :], (8, width)) for row in range(4)]
            top = jnp.where(sub8, lines[0], lines[1])
            low = jnp.where(sub8, lines[2], lines[3])
            blk[code * entries + spot] = jnp.concatenate([top, low], axis=0).astype(bf16)
        return carry

    lax.fori_loop(0, CODES, build, 0)

    tiles = []
    start = 0
    while start < orbits:
        size = 2 if orbits - start in (2, 4) else 3
        tiles.append((start, min(size, orbits - start)))
        start += size

    for step in range(STEPS):
        current = vec_ref if step == 0 else state.at[(step - 1) % 2]
        for copy in copies:
            copy.wait()
        for which, base in enumerate((3, 0)):
            side[which, 0:8] = cols_in[step, base + 2].astype(f32)[8:16]
            side[which, 8:24] = cols_in[step, base].astype(f32)
            side[which, 24:32] = cols_in[step, base + 1].astype(f32)[0:8]

        def spread(pair, carry):
            above = rows_in[step, 1, pair].astype(f32)
            below = rows_in[step, 0, pair].astype(f32)
            for half in range(2):
                field = 2 * pair + half
                spot = 2 * field
                centre = jnp.concatenate(
                    [above[8 * half : 8 * half + 8], current[field], below[8 * half : 8 * half + 8]],
                    axis=0,
                )
                left = pltpu.roll(side[0], lax.rem(LANES - 2 - spot + LANES, LANES), 1)
                right = pltpu.roll(side[1], lax.rem(LANES - spot, LANES), 1)
                for shift, tile in enumerate(shifts(centre, left, right)):
                    for chunk in range(chunks):
                        cols = slice(chunk * LANES, (chunk + 1) * LANES)
                        tmp[half, shift, chunk] = tile[:, cols]
                        for lift in range(5):
                            moved[lift * 5 + shift, field, :, cols] = tmp[
                                half, shift, chunk, 4 * lift : 4 * lift + 16
                            ].astype(bf16)
            return carry

        lax.fori_loop(0, fields // 2, spread, 0)

        target = out_ref if step == STEPS - 1 else state.at[step % 2]
        previous = vec_ref if step == 1 else state.at[step % 2]
        for chunk in range(chunks):
            cols = slice(chunk * LANES, (chunk + 1) * LANES)
            for start, size in tiles:

                def gather(code, sums):
                    parts = [[None, None] for _ in range(size * groups)]
                    for other in range(orbits):
                        chain = 0 if other < 7 else 1
                        fields_in = [moved[code, g * orbits + other, :, cols] for g in range(groups)]
                        for k in range(size):
                            entry = blk[code * entries + (start + k) * orbits + other, :, cols]
                            for g in range(groups):
                                part = parts[k * groups + g]
                                term = entry * fields_in[g]
                                part[chain] = term if part[chain] is None else part[chain] + term
                    return tuple(
                        total + (part[0] + part[1]).astype(f32) for total, part in zip(sums, parts)
                    )

                zero = jnp.zeros((16, LANES), f32)
                sums = lax.fori_loop(0, CODES, gather, (zero,) * (size * groups))
                for k in range(size):
                    for g in range(groups):
                        field = g * orbits + start + k
                        value = sums[k * groups + g]
                        if step:
                            value = 2.0 * value - previous[field, :, cols]
                        target[field, :, cols] = value
        if step < STEPS - 1:
            copies = send_state(target, step + 1)


def body(vectors, features, gains, edge_weight, energies, neighbours, species):
    count, orbits, rows, width = vectors.shape
    groups = count // 4
    channels = features.shape[0]
    entries = orbits * orbits
    padded = -(-entries // 16) * 16
    fields = groups * orbits
    f32, bf16 = jnp.float32, jnp.bfloat16
    vec = vectors.reshape(groups, 4, orbits, rows, width).transpose(0, 2, 3, 1, 4)
    vec = vec.reshape(fields, rows * 4, width)
    feat = features.transpose(1, 0, 2)
    gain = jnp.pad(gains.T, ((0, 0), (0, LANES - gains.shape[0])))
    weight = jnp.pad(edge_weight.T, ((0, padded - entries), (0, 0)))
    onsite = jnp.zeros((rows, orbits, width), f32)
    for kind in range(energies.shape[1]):
        onsite = jnp.where(species[:, None] == kind, energies[:, kind][None, :, None], onsite)
    vmem = pl.BlockSpec(memory_space=pltpu.VMEM)
    out = pl.pallas_call(
        functools.partial(kernel, orbits, groups),
        out_shape=jax.ShapeDtypeStruct(vec.shape, f32),
        in_specs=[vmem] * 6,
        out_specs=vmem,
        scratch_shapes=[
            pltpu.VMEM((CODES * entries, 16, width), bf16),
            pltpu.VMEM((CODES, fields, 16, width), bf16),
            pltpu.VMEM((2, fields, 16, width), f32),
            pltpu.VMEM((5, rows + 4, channels, width), bf16),
            pltpu.VMEM((rows, padded, width), f32),
            pltpu.VMEM((2, 5, width // LANES, 32, LANES), f32),
            pltpu.VMEM((2, channels, LANES), bf16),
            pltpu.VMEM((2, 2, channels, width), bf16),
            pltpu.VMEM((6, channels, LANES), bf16),
            pltpu.VMEM((STEPS, 2, fields // 2, 16, width), bf16),
            pltpu.VMEM((STEPS, 2, 16, LANES), bf16),
            pltpu.VMEM((STEPS, 2, fields // 2, 16, width), bf16),
            pltpu.VMEM((STEPS, 6, 16, LANES), bf16),
            pltpu.VMEM((2, 32, LANES), f32),
            pltpu.SemaphoreType.DMA((STEPS + 1, len(ROUTES))),
            pltpu.SemaphoreType.DMA((STEPS + 1, len(ROUTES))),
        ],
        compiler_params=pltpu.CompilerParams(
            collective_id=0, has_side_effects=True, vmem_limit_bytes=62 * 1024 * 1024
        ),
        cost_estimate=pl.CostEstimate(
            flops=STEPS * 2 * CODES * entries * count * rows * width,
            bytes_accessed=4 * 1024 * 1024,
            transcendentals=0,
        ),
    )(vec, feat, gain, weight, onsite, neighbours)
    out = out.reshape(groups, orbits, rows, 4, width).transpose(0, 3, 1, 2, 4)
    return out.reshape(vectors.shape)


def solution(mesh):
    return jax.shard_map(
        body,
        mesh=mesh,
        in_specs=(
            P(None, None, "gx", "gy"),
            P(None, "gx", "gy"),
            P(),
            P(),
            P(),
            P(None, "gx", "gy"),
            P("gx", "gy"),
        ),
        out_specs=P(None, None, "gx", "gy"),
        check_vma=False,
    )
```
